256 devices in a mesh: dp: 16 (over y, x), emb: 8 (over z), section: 2 (over core).
Axes of the slice: x: 4, y: 4, z: 8, core: 2. Of those that a mesh axis runs over, the one named last changes fastest.
Arguments:
- events: bfloat16 [8192, 64, 4, 256], P(('emb', 'section'), 'dp'), may hold values from -6 to 6
- counts: int32 [8192, 64], P(('emb', 'section'), 'dp'), may hold values from 1 to 4
- live: int32 [8192, 64], P(('emb', 'section'), 'dp'), may hold values 0 or 1
- enc_weight: bfloat16 [256, 256], replicated, may hold values from -0.375 to 0.375
- fm_proj: bfloat16 [64, 32], replicated, may hold values from -0.75 to 0.75
- ln_gain: float32 [2048], replicated, may hold values from 0.1 to 1.9
- w_hidden: bfloat16 [2048, 4096], P(None, ('emb', 'section')), may hold values from -0.125 to 0.125
- w_out: bfloat16 [4096, 32, 256], P(None, None, ('emb', 'section')), may hold values from -0.09375 to 0.09375
- lcb_weight: bfloat16 [32, 64], replicated, may hold values from -0.75 to 0.75
- out_gain: float32 [256], P(('emb', 'section')), may hold values from 0.1 to 1.9
Outputs:
- layer_out: bfloat16 [8192, 64, 256], P('dp', None, ('emb', 'section'))
The draws below stay inside these ranges and needn't reach their ends.
All inputs are finite; a program needn't handle non-finite values. No bound on the sum of `live` on one device may be relied on, other than what follows from the above.
Results may differ from the reference program's by a relative error of at most 0.013.
Values may be sent and summed in bfloat16 or wider, within the bound.
No kernel may reach another device: no remote copies, remote signals or barrier semaphores. Data moves between devices by JAX's collectives and lax.ppermute only.
A program may use at most 128 MiB of HBM per device.

```python
import jax
import jax.numpy as jnp
from jax import lax

D = 256
N_SESS = 64
SLOTS = 4
K = 32
NF = 32
NL = 32
H = 4096
USR_DEV = 512
USERS = 8192


def touch_ends(values, key, least, largest):
    dims = values.shape
    spot = [jax.random.randint(jax.random.fold_in(key, axis), (), 0, dims[axis]) for axis in range(len(dims))]
    values = values.at[tuple(spot)].set(least)
    longest = dims.index(max(dims))
    spot[longest] = (spot[longest] + 1) % dims[longest]
    return values.at[tuple(spot)].set(largest)


def steps_of(own_key, dims, pieces, low, largest):
    level, own = 1.0, jax.random.fold_in(own_key, 6)
    for axis_at, blocks in pieces:
        heights = jnp.exp(jax.random.uniform(jax.random.fold_in(own, axis_at), (blocks,), jnp.float32, low / len(pieces), largest / len(pieces)))
        level = level * jnp.repeat(heights, dims[axis_at] // blocks).reshape([-1 if axis == axis_at else 1 for axis in range(len(dims))])
    return level


def centred(own_key, shape, width, reach, cuts=(), kind=jnp.bfloat16):
    entries = jax.random.normal(own_key, shape, jnp.float32) * width
    if len(cuts) > 0:
        entries = steps_of(own_key, shape, cuts, -0.22, 0.18) * entries
    return jnp.clip(entries, min=-reach, max=reach).astype(kind)


def setup_inputs(seed: int = 0) -> dict:
    arg_keys = jax.random.split(jax.random.key(seed), 11)
    events = centred(arg_keys[0], (USERS, N_SESS, SLOTS, D), 1.0, 6.0, ((0, 16), (1, 16)))
    counts = touch_ends(jax.random.randint(arg_keys[1], (USERS, N_SESS), 1, SLOTS + 1), jax.random.fold_in(arg_keys[1], 1), 1, SLOTS).astype(jnp.int32)
    live = touch_ends((jax.random.randint(arg_keys[2], (USERS, N_SESS), 0, 4) < 3).astype(jnp.int32), jax.random.fold_in(arg_keys[2], 1), 0, 1)
    enc_weight = centred(arg_keys[3], (D, D), D ** -0.5, 0.375)
    fm_proj = centred(arg_keys[4], (N_SESS, K), N_SESS ** -0.5, 0.75)
    ln_gain = jnp.clip(1.0 + 0.18 * jax.random.normal(arg_keys[5], (N_SESS * K,), jnp.float32), 0.1, 1.9)
    w_hidden = centred(arg_keys[6], (N_SESS * K, H), (N_SESS * K) ** -0.5, 0.125, ((1, 16),))
    w_out = centred(arg_keys[7], (H, NF, D), H ** -0.5, 0.09375, ((2, 16),))
    lcb_weight = centred(arg_keys[8], (NL, N_SESS), N_SESS ** -0.5, 0.75)
    out_gain = jnp.clip(1.0 + 0.18 * jax.random.normal(arg_keys[9], (D,), jnp.float32), 0.1, 1.9)
    return dict(events=events, counts=counts, live=live, enc_weight=enc_weight, fm_proj=fm_proj, ln_gain=ln_gain, w_hidden=w_hidden, w_out=w_out, lcb_weight=lcb_weight, out_gain=out_gain)


def layer_norm_rows(values, gain):
    center = lax.optimization_barrier(jnp.mean(values, axis=-1, keepdims=True))
    meansq = lax.optimization_barrier(jnp.mean(values * values, axis=-1, keepdims=True))
    return (values - center) * lax.rsqrt(meansq - center * center + 1e-05) * gain

def user_block(blocks, enc_weight, fm_proj, ln_gain, w_hidden, w_out, lcb_weight, out_gain):
    events, counts, live = blocks
    inside = (jnp.arange(SLOTS, dtype=jnp.int32)[None, None, :] < counts[:, :, None]).astype(jnp.float32)
    session_sums = jnp.einsum('usj,usjd->usd', inside, events.astype(jnp.float32))
    pooled = (session_sums / counts[:, :, None].astype(jnp.float32)).astype(jnp.bfloat16)
    encoded = jnp.dot(pooled.reshape(-1, D), enc_weight, preferred_element_type=jnp.float32).reshape(-1, N_SESS, D)
    session = (encoded * live[:, :, None].astype(jnp.float32)).astype(jnp.bfloat16)
    session_wide = session.astype(jnp.float32)
    reduced = jnp.einsum('und,nk->udk', session_wide, fm_proj.astype(jnp.float32)).astype(jnp.bfloat16)
    fm_rows = jnp.einsum('und,udk->unk', session_wide, reduced.astype(jnp.float32)).reshape(-1, N_SESS * K)
    normed = layer_norm_rows(fm_rows, ln_gain).astype(jnp.bfloat16)
    hidden = jnp.maximum(jnp.dot(normed, w_hidden, preferred_element_type=jnp.float32), 0.0).astype(jnp.bfloat16)
    fm_out = jnp.dot(hidden, w_out.reshape(H, NF * D), preferred_element_type=jnp.float32).reshape(-1, NF, D)
    compressed = jnp.einsum('mn,und->umd', lcb_weight.astype(jnp.float32), session_wide)
    summed = jnp.concatenate([fm_out, compressed], axis=1) + session_wide
    return layer_norm_rows(summed, out_gain).astype(jnp.bfloat16)

def reference(events, counts, live, enc_weight, fm_proj, ln_gain, w_hidden, w_out, lcb_weight, out_gain):
    groups = USERS // USR_DEV
    blocks = (events.reshape(groups, USR_DEV, N_SESS, SLOTS, D), counts.reshape(groups, USR_DEV, N_SESS), live.reshape(groups, USR_DEV, N_SESS))
    result = lax.map(lambda item: user_block(item, enc_weight, fm_proj, ln_gain, w_hidden, w_out, lcb_weight, out_gain), blocks)
    return result.reshape(USERS, N_SESS, D)
```

```python
import functools

import jax
import jax.numpy as jnp
from jax import lax
from jax.experimental import pallas as pl
from jax.experimental.pallas import tpu as pltpu
from jax.sharding import PartitionSpec as P

D = 256
N = 64
K = 32
U = 32
Z = 8
F32 = jnp.float32
BF = jnp.bfloat16
VMEM = pl.BlockSpec(memory_space=pltpu.VMEM)
SMEM = pl.BlockSpec(memory_space=pltpu.SMEM)
PARAMS = pltpu.CompilerParams(vmem_limit_bytes=48 * 1024 * 1024)
UP = [(i, (i + 1) % Z) for i in range(Z)]
DOWN = [(i, (i - 1) % Z) for i in range(Z)]
SWAP = [(0, 1), (1, 0)]
LANES = ((1,), (1,)), ((), ())


def dot_t(a, b):
    return lax.dot_general(a, b, LANES, preferred_element_type=F32)


def fm_kernel(x_ref, mix_ref, gain_ref, normed_ref, comp_a, comp_b, xa, xb, ts):
    xa[...] = x_ref[:, :128].astype(F32)
    xb[...] = x_ref[:, 128:].astype(F32)
    for u in range(U):
        sides = [
            jnp.concatenate(
                [xs[pl.ds(first * U + u, 16, stride=4 * U), :] for first in range(4)], axis=0
            )
            for xs in (xa, xb)
        ]
        xu = jnp.concatenate(sides, axis=1).astype(BF)
        both = jnp.dot(mix_ref[...], xu, preferred_element_type=F32)
        comp_a[pl.ds(u, 32, stride=U), :] = both[K:, :128]
        comp_b[pl.ds(u, 32, stride=U), :] = both[K:, 128:]
        fm = dot_t(xu, both[:K].astype(BF))
        ts[pl.ds(u, 16, stride=U), :] = jnp.concatenate(
            [fm[16 * i : 16 * i + 16] for i in range(4)], axis=1
        )
    t = ts[...].reshape(16, U, 128)
    m = jnp.sum(jnp.sum(t, axis=0), axis=-1, keepdims=True) / (N * K)
    q = jnp.sum(jnp.sum(t * t, axis=0), axis=-1, keepdims=True) / (N * K)
    scale = lax.rsqrt(q - m * m + 1e-05)
    for g in range(16):
        normed_ref[:, g * 128 : g * 128 + 128] = (
            (t[g] - m) * scale * gain_ref[g : g + 1, :]
        ).astype(BF)


def slice_kernel(x_ref, comp_a, comp_b, perm_ref, out_ref, cut):
    y = jnp.concatenate([comp_a[...], comp_b[...]], axis=1) + x_ref[32 * U :, :].astype(F32)
    m = jnp.mean(y, axis=-1, keepdims=True)
    q = jnp.mean(y * y, axis=-1, keepdims=True)
    y = ((y - m) * lax.rsqrt(q - m * m + 1e-05)).astype(BF)
    for big in range(8):
        for t in range(2):
            for i in range(8):
                row = (8 * big + i) * U
                if big < 4:
                    piece = x_ref[row : row + U, t * 128 : t * 128 + 128]
                else:
                    row -= 32 * U
                    piece = y[row : row + U, t * 128 : t * 128 + 128]
                at = (2 * big + t) * U
                cut[at : at + U, i * 128 : i * 128 + 128] = piece
    o = jnp.dot(cut[...], perm_ref[...], preferred_element_type=F32).astype(BF)
    for big in range(8):
        for t in range(2):
            at = (2 * big + t) * U
            for e in range(8):
                out_ref[t * 8 + e, :, big * 128 : big * 128 + 128] = o[
                    at : at + U, e * 128 : e * 128 + 128
                ]


def hidden_kernel(at_ref, *refs):
    chunks, (own, other, out_ref, held) = refs[:9], refs[9:]
    z, c = at_ref[0], at_ref[1]
    for k, ref in zip((0, 7, 6, 5, 1, 2, 3), chunks[:7]):
        held[pl.ds(pl.multiple_of(lax.rem(z + k, Z) * U, U), U), :] = ref[...]
    half = pl.multiple_of(lax.rem(z + 4, Z) * U, U)
    held[pl.ds(half, U // 2), :] = chunks[7][...]
    held[pl.ds(half + U // 2, U // 2), :] = chunks[8][...]
    for where, w in ((c, own), (1 - c, other)):
        h = jnp.dot(held[...], w[...], preferred_element_type=F32)
        out_ref[:, pl.ds(pl.multiple_of(where * 256, 256), 256)] = jnp.maximum(h, 0.0).astype(BF)


def out_kernel(at_ref, *refs):
    chunks = refs[:9]
    own, other, s_own, s_other, o_own, o_other, t1_ref, t2_ref = refs[9:]
    z = at_ref[0]
    users, wide = o_own.shape
    mask = (
        lax.broadcasted_iota(jnp.int32, (8, wide), 1) // 16
        == lax.broadcasted_iota(jnp.int32, (8, wide), 0)
    ).astype(BF)
    t1 = jnp.zeros((8, users), F32)
    t2 = jnp.zeros((8, users), F32)
    for w, s, o in ((own, s_own, o_own), (other, s_other, o_other)):
        acc = s[:, 0].reshape(users, wide).astype(F32)
        for k, ref in zip((0, 7, 6, 5, 1, 2, 3), chunks[:7]):
            at = pl.multiple_of(lax.rem(z + k, Z) * 512, 512)
            acc += dot_t(ref[...], w[:, pl.ds(at, 512)])
        at = pl.multiple_of(lax.rem(z + 4, Z) * 512, 512)
        acc += jnp.concatenate(
            [dot_t(chunks[7][...], w[:, pl.ds(at, 512)]), dot_t(chunks[8][...], w[:, pl.ds(at, 512)])],
            axis=0,
        )
        o[...] = acc
        for v, which in ((acc, 0), (acc * acc, 1)):
            high = v.astype(BF)
            low = (v - high.astype(F32)).astype(BF)
            part = dot_t(mask, high) + dot_t(mask, low)
            if which:
                t2 += part
            else:
                t1 += part
    t1_ref[...] = t1
    t2_ref[...] = t2


def scale_kernel(c_ref, s_own, s_other, tot_ref, slices_ref, o_own, o_other):
    c = c_ref[1]
    users = s_own.shape[0]
    m = tot_ref[:32, :] / D
    q = tot_ref[32:, :] / D
    r = lax.rsqrt(q - m * m + 1e-05)
    spread = (
        lax.broadcasted_iota(jnp.int32, (32, 512), 1) // 16
        == lax.broadcasted_iota(jnp.int32, (32, 512), 0)
    ).astype(BF)

    def widen(v):
        high = v.astype(BF)
        low = (v - high.astype(F32)).astype(BF)
        dims = ((0,), (0,)), ((), ())
        return lax.dot_general(high, spread, dims, preferred_element_type=F32) + lax.dot_general(
            low, spread, dims, preferred_element_type=F32
        )

    m, r = widen(m), widen(r)
    for which, s, o in ((c, s_own, o_own), (1 - c, s_other, o_other)):
        o[:, :512] = ((s[...] - m) * r).astype(BF)
        o[:, 512:] = slices_ref[:, pl.ds(which, 1), :, 512:].reshape(users, 512)


def finish_kernel(v_ref, gain_ref, o_ref):
    v = v_ref[...].astype(F32).T * gain_ref[...]
    o_ref[...] = v.astype(BF)


def ring(v):
    half = v.shape[0] // 2
    ups, downs = [v], [v]
    for _ in range(3):
        ups.append(lax.ppermute(ups[-1], "emb", UP))
        downs.append(lax.ppermute(downs[-1], "emb", DOWN))
    last = [
        lax.ppermute(ups[-1][:half], "emb", UP),
        lax.ppermute(downs[-1][half:], "emb", DOWN),
    ]
    return [*ups, *downs[1:], *last]


def shards(
    events, counts, live, enc_weight, fm_proj, ln_gain, w_hidden, w_out, lcb_weight, out_gain
):
    users_enc, sess_dev, slot_count, full_width = events.shape
    z, c = lax.axis_index("emb"), lax.axis_index("section")
    place = jnp.stack([z, c]).astype(jnp.int32)
    w_hidden_other = lax.ppermute(w_hidden, "section", SWAP)
    w_own = jnp.transpose(w_out, (1, 2, 0)).reshape(512, -1)
    w_other = lax.ppermute(w_own, "section", SWAP)

    inside = (lax.broadcasted_iota(jnp.int32, (1, 1, slot_count), 2) < counts[:, :, None]).astype(BF)
    session_sums = jnp.einsum("usj,usjd->usd", inside, events, preferred_element_type=F32)
    pooled = (session_sums / counts[:, :, None].astype(F32)).astype(BF)
    encoded = jnp.dot(pooled.reshape(-1, full_width), enc_weight, preferred_element_type=F32)
    encoded = encoded.reshape(users_enc, sess_dev, full_width)
    session = (encoded * live[:, :, None].astype(F32)).astype(BF)
    chunks = jnp.transpose(session.reshape(16, U, sess_dev, D), (0, 2, 1, 3))
    x = lax.all_to_all(chunks, "dp", 0, 0, tiled=True).reshape(N * U, D)

    mix = jnp.concatenate([fm_proj.T, lcb_weight], axis=0)
    mix = jnp.transpose(mix.reshape(64, 16, 4), (0, 2, 1)).reshape(64, 64)
    normed, comp_a, comp_b = pl.pallas_call(
        fm_kernel,
        out_shape=[jax.ShapeDtypeStruct((U, N * K), BF)]
        + [jax.ShapeDtypeStruct((32 * U, 128), F32)] * 2,
        in_specs=[VMEM] * 3,
        out_specs=[VMEM] * 3,
        scratch_shapes=[pltpu.VMEM((N * U, 128), F32)] * 2 + [pltpu.VMEM((16 * U, 128), F32)],
        compiler_params=PARAMS,
        name="fm_rows",
    )(x, mix, ln_gain.reshape(16, 128))

    place_in = lax.broadcasted_iota(jnp.int32, (1024, 1), 0)
    i, e, f = place_in // 128, (place_in // 16) % 8, place_in % 16
    perm = (e * 128 + i * 16 + f == lax.broadcasted_iota(jnp.int32, (1, 1024), 1)).astype(BF)
    slices = pl.pallas_call(
        slice_kernel,
        out_shape=jax.ShapeDtypeStruct((16, U, 1024), BF),
        in_specs=[VMEM] * 4,
        out_specs=VMEM,
        scratch_shapes=[pltpu.VMEM((512, 1024), BF)],
        compiler_params=PARAMS,
        name="slices",
    )(x, comp_a, comp_b, perm)
    slices = lax.all_to_all(slices.reshape(Z, 2 * U, 1024), "emb", 0, 0, tiled=True)
    slices = slices.reshape(Z, 2, U, 1024)

    gathered = ring(normed)
    hidden = pl.pallas_call(
        hidden_kernel,
        out_shape=jax.ShapeDtypeStruct((Z * U, 512), BF),
        in_specs=[SMEM] + [VMEM] * 11,
        out_specs=VMEM,
        scratch_shapes=[pltpu.VMEM((Z * U, N * K), BF)],
        compiler_params=PARAMS,
        name="hidden",
    )(place, *gathered, w_hidden, w_hidden_other)

    gathered = ring(hidden)
    users = Z * U
    whole = [pl.BlockSpec(v.shape, lambda i, s: (0, 0)) for v in gathered]
    s_own, s_other, t1, t2 = pl.pallas_call(
        out_kernel,
        grid_spec=pltpu.PrefetchScalarGridSpec(
            num_scalar_prefetch=1,
            grid=(4,),
            in_specs=whole
            + [pl.BlockSpec((128, 4096), lambda i, s: (i, 0))] * 2
            + [
                pl.BlockSpec((Z, 1, U, 128), lambda i, s: (0, s[1], 0, i)),
                pl.BlockSpec((Z, 1, U, 128), lambda i, s: (0, 1 - s[1], 0, i)),
            ],
            out_specs=[pl.BlockSpec((users, 128), lambda i, s: (0, i))] * 2
            + [pl.BlockSpec((8, users), lambda i, s: (i, 0))] * 2,
        ),
        out_shape=[jax.ShapeDtypeStruct((users, 512), F32)] * 2
        + [jax.ShapeDtypeStruct((32, users), F32)] * 2,
        compiler_params=PARAMS,
        name="fm_out",
    )(place, *gathered, w_own, w_other, slices, slices)

    totals = jnp.concatenate([t1, t2], axis=0)
    for bit in (1, 2, 4):
        totals = totals + lax.ppermute(totals, "emb", [(i, i ^ bit) for i in range(Z)])

    o_own, o_other = pl.pallas_call(
        scale_kernel,
        out_shape=[jax.ShapeDtypeStruct((users, 1024), BF)] * 2,
        in_specs=[SMEM] + [VMEM] * 4,
        out_specs=[VMEM] * 2,
        compiler_params=PARAMS,
        name="scale",
    )(place, s_own, s_other, totals, slices)
    came = lax.ppermute(o_other, "section", SWAP)
    o_own, came = o_own.reshape(Z, 1, U, 1024), came.reshape(Z, 1, U, 1024)
    send = jnp.where(
        c == 0, jnp.concatenate([o_own, came], axis=1), jnp.concatenate([came, o_own], axis=1)
    )
    out = lax.all_to_all(send.reshape(16, U, 1024), "dp", 0, 0, tiled=True)
    gain = jnp.tile(out_gain, 64).reshape(1024, 1)
    out = pl.pallas_call(
        finish_kernel,
        out_shape=jax.ShapeDtypeStruct((1024, 512), BF),
        in_specs=[VMEM] * 2,
        out_specs=VMEM,
        compiler_params=PARAMS,
        name="finish",
    )(out.reshape(512, 1024), gain)
    return jnp.transpose(out.reshape(64, 16, 512), (2, 0, 1))


def solution(mesh):
    in_specs = (
        P(("emb", "section"), "dp", None, None),
        P(("emb", "section"), "dp"),
        P(("emb", "section"), "dp"),
        P(),
        P(),
        P(),
        P(None, ("emb", "section")),
        P(None, None, ("emb", "section")),
        P(),
        P(("emb", "section")),
    )
    out_specs = P("dp", None, ("emb", "section"))
    return jax.shard_map(shards, mesh=mesh, in_specs=in_specs, out_specs=out_specs, check_vma=False)
```

```python
import functools

import jax
import jax.numpy as jnp
from jax import lax
from jax.experimental import pallas as pl
from jax.experimental.pallas import tpu as pltpu
from jax.sharding import PartitionSpec as P

D = 256
N = 64
K = 32
U = 32
Z = 8
F32 = jnp.float32
BF = jnp.bfloat16
VMEM = pl.BlockSpec(memory_space=pltpu.VMEM)
SMEM = pl.BlockSpec(memory_space=pltpu.SMEM)
PARAMS = pltpu.CompilerParams(vmem_limit_bytes=48 * 1024 * 1024)
UP = [(i, (i + 1) % Z) for i in range(Z)]
DOWN = [(i, (i - 1) % Z) for i in range(Z)]
SWAP = [(0, 1), (1, 0)]
LANES = ((1,), (1,)), ((), ())


def dot_t(a, b):
    return lax.dot_general(a, b, LANES, preferred_element_type=F32)


def fm_kernel(x_ref, mix_ref, gain_ref, normed_ref, comp_a, comp_b, xa, xb, ts):
    xa[...] = x_ref[:, :128].astype(F32)
    xb[...] = x_ref[:, 128:].astype(F32)
    for u in range(U):
        sides = [
            jnp.concatenate(
                [xs[pl.ds(first * U + u, 16, stride=4 * U), :] for first in range(4)], axis=0
            )
            for xs in (xa, xb)
        ]
        xu = jnp.concatenate(sides, axis=1).astype(BF)
        both = jnp.dot(mix_ref[...], xu, preferred_element_type=F32)
        comp_a[pl.ds(u, 32, stride=U), :] = both[K:, :128]
        comp_b[pl.ds(u, 32, stride=U), :] = both[K:, 128:]
        fm = dot_t(xu, both[:K].astype(BF))
        ts[pl.ds(u, 16, stride=U), :] = jnp.concatenate(
            [fm[16 * i : 16 * i + 16] for i in range(4)], axis=1
        )
    t = ts[...].reshape(16, U, 128)
    m = jnp.sum(jnp.sum(t, axis=0), axis=-1, keepdims=True) / (N * K)
    q = jnp.sum(jnp.sum(t * t, axis=0), axis=-1, keepdims=True) / (N * K)
    scale = lax.rsqrt(q - m * m + 1e-05)
    for g in range(16):
        normed_ref[:, g * 128 : g * 128 + 128] = (
            (t[g] - m) * scale * gain_ref[g : g + 1, :]
        ).astype(BF)


def slice_kernel(at_ref, x_ref, comp_a, comp_b, perm_ref, *refs):
    outs, (cut, made) = refs[:Z], refs[Z:]
    y = jnp.concatenate([comp_a[...], comp_b[...]], axis=1) + x_ref[32 * U :, :].astype(F32)
    m = jnp.mean(y, axis=-1, keepdims=True)
    q = jnp.mean(y * y, axis=-1, keepdims=True)
    y = ((y - m) * lax.rsqrt(q - m * m + 1e-05)).astype(BF)
    for big in range(8):
        for t in range(2):
            for i in range(8):
                row = (8 * big + i) * U
                if big < 4:
                    piece = x_ref[row : row + U, t * 128 : t * 128 + 128]
                else:
                    row -= 32 * U
                    piece = y[row : row + U, t * 128 : t * 128 + 128]
                at = (2 * big + t) * U
                cut[at : at + U, i * 128 : i * 128 + 128] = piece
    o = jnp.dot(cut[...], perm_ref[...], preferred_element_type=F32).astype(BF)
    for big in range(8):
        for t in range(2):
            at = (2 * big + t) * U
            for e in range(8):
                made[t * 4 + e // 2, e % 2, :, big * 128 : big * 128 + 128] = o[
                    at : at + U, e * 128 : e * 128 + 128
                ]
    for k, ref in enumerate(outs):
        ref[...] = made[lax.rem(at_ref[0] + k, Z)]


def hidden_kernel(at_ref, *refs):
    chunks, (own, other, out_ref, held) = refs[:9], refs[9:]
    z, c = at_ref[0], at_ref[1]
    for k, ref in zip((0, 7, 6, 5, 1, 2, 3), chunks[:7]):
        held[pl.ds(pl.multiple_of(lax.rem(z + k, Z) * U, U), U), :] = ref[...]
    half = pl.multiple_of(lax.rem(z + 4, Z) * U, U)
    held[pl.ds(half, U // 2), :] = chunks[7][...]
    held[pl.ds(half + U // 2, U // 2), :] = chunks[8][...]
    for where, w in ((c, own), (1 - c, other)):
        h = jnp.dot(held[...], w[...], preferred_element_type=F32)
        out_ref[:, pl.ds(pl.multiple_of(where * 256, 256), 256)] = jnp.maximum(h, 0.0).astype(BF)


def part_kernel(n, at_ref, *refs):
    chunks, weights = refs[:n], refs[n : 3 * n]
    sums, outs = refs[3 * n : -2], refs[-2:]
    for side, out in enumerate(outs):
        acc = sum(dot_t(chunks[i][...], weights[2 * i + side][...]) for i in range(n))
        out[...] = acc + sums[side][...] if sums else acc


def part(place, blocks, weights, sums):
    n = len(blocks)

    def columns(k):
        return pl.BlockSpec((512, 512), lambda i, at: (0, lax.rem(at[0] + k, Z)))

    whole = pl.BlockSpec((Z * U, 512), lambda i, at: (0, 0))
    return pl.pallas_call(
        functools.partial(part_kernel, n),
        grid_spec=pltpu.PrefetchScalarGridSpec(
            num_scalar_prefetch=1,
            grid=(1,),
            in_specs=[whole] * n
            + [columns(k) for k, _ in blocks for _ in range(2)]
            + [whole] * len(sums),
            out_specs=[whole] * 2,
        ),
        out_shape=[jax.ShapeDtypeStruct((Z * U, 512), F32)] * 2,
        compiler_params=PARAMS,
        cost_estimate=pl.CostEstimate(
            flops=n * 2 * 2 * 256 * 512 * 512, bytes_accessed=n * 2**20, transcendentals=0
        ),
        name="fm_out_part",
    )(place, *[v for _, v in blocks], *[w for _ in blocks for w in weights], *sums)


def out_kernel(at_ref, low, high, w_own, w_other, a_own, a_other, *refs):
    slices, (o_own, o_other, tot_ref) = refs[:Z], refs[Z:]
    z, c = at_ref[0], at_ref[1]
    half = low.shape[0]
    for which, w, a, o in ((c, w_own, a_own, o_own), (1 - c, w_other, a_other, o_other)):
        o[:half] = a[:half] + dot_t(low[...], w[...])
        o[half:] = a[half:] + dot_t(high[...], w[...])
        for k, ref in enumerate(slices):
            rows = pl.ds(pl.multiple_of(lax.rem(z + Z - k, Z) * U, U), U)
            o[rows, :] += ref[pl.ds(which, 1), :, :512][0].astype(F32)
    mask = (
        lax.broadcasted_iota(jnp.int32, (32, 512), 1) // 16
        == lax.broadcasted_iota(jnp.int32, (32, 512), 0)
    ).astype(BF)
    x, y = o_own[...], o_other[...]
    for at, v in ((0, x + y), (32, x * x + y * y)):
        upper = v.astype(BF)
        rest = (v - upper.astype(F32)).astype(BF)
        tot_ref[at : at + 32, :] = dot_t(mask, upper) + dot_t(mask, rest)


def scale_kernel(at_ref, s_own, s_other, tot_ref, *refs):
    slices, (o_own, o_other) = refs[:Z], refs[Z:]
    z, c = at_ref[0], at_ref[1]
    m = tot_ref[:32, :] / D
    q = tot_ref[32:, :] / D
    r = lax.rsqrt(q - m * m + 1e-05)
    spread = (
        lax.broadcasted_iota(jnp.int32, (32, 512), 1) // 16
        == lax.broadcasted_iota(jnp.int32, (32, 512), 0)
    ).astype(BF)

    def widen(v):
        high = v.astype(BF)
        low = (v - high.astype(F32)).astype(BF)
        dims = ((0,), (0,)), ((), ())
        return lax.dot_general(high, spread, dims, preferred_element_type=F32) + lax.dot_general(
            low, spread, dims, preferred_element_type=F32
        )

    m, r = widen(m), widen(r)
    for which, s, o in ((c, s_own, o_own), (1 - c, s_other, o_other)):
        o[:, :512] = ((s[...] - m) * r).astype(BF)
        for k, ref in enumerate(slices):
            rows = pl.ds(pl.multiple_of(lax.rem(z + Z - k, Z) * U, U), U)
            o[rows, 512:] = ref[pl.ds(which, 1), :, 512:][0]


def finish_kernel(v_ref, gain_ref, o_ref):
    v = v_ref[...].astype(F32).T * gain_ref[...]
    o_ref[...] = v.astype(BF)


def step(up, down):
    return lax.ppermute(up, "emb", UP), lax.ppermute(down, "emb", DOWN)


def after(value, event):
    return lax.optimization_barrier((value, event))


def shards(
    events, counts, live, enc_weight, fm_proj, ln_gain, w_hidden, w_out, lcb_weight, out_gain
):
    users_enc, sess_dev, slot_count, full_width = events.shape
    z, c = lax.axis_index("emb"), lax.axis_index("section")
    place = jnp.stack([z, c]).astype(jnp.int32)
    w_hidden_other = lax.ppermute(w_hidden, "section", SWAP)
    w_own = jnp.transpose(w_out, (1, 2, 0)).reshape(512, -1)
    w_other = lax.ppermute(w_own, "section", SWAP)

    inside = (lax.broadcasted_iota(jnp.int32, (1, 1, slot_count), 2) < counts[:, :, None]).astype(BF)
    session_sums = jnp.einsum("usj,usjd->usd", inside, events, preferred_element_type=F32)
    share_of = live.astype(F32) / counts.astype(F32)
    pooled = (session_sums * share_of[:, :, None]).astype(BF)
    encoded = jnp.dot(pooled.reshape(-1, full_width), enc_weight, preferred_element_type=F32)
    session = encoded.reshape(users_enc, sess_dev, full_width).astype(BF)
    chunks = jnp.transpose(session.reshape(16, U, sess_dev, D), (0, 2, 1, 3))
    x = lax.all_to_all(chunks, "dp", 0, 0, tiled=True).reshape(N * U, D)

    mix = jnp.concatenate([fm_proj.T, lcb_weight], axis=0)
    mix = jnp.transpose(mix.reshape(64, 16, 4), (0, 2, 1)).reshape(64, 64)
    normed, comp_a, comp_b = pl.pallas_call(
        fm_kernel,
        out_shape=[jax.ShapeDtypeStruct((U, N * K), BF)]
        + [jax.ShapeDtypeStruct((32 * U, 128), F32)] * 2,
        in_specs=[VMEM] * 3,
        out_specs=[VMEM] * 3,
        scratch_shapes=[pltpu.VMEM((N * U, 128), F32)] * 2 + [pltpu.VMEM((16 * U, 128), F32)],
        compiler_params=PARAMS,
        name="fm_rows",
    )(x, mix, ln_gain.reshape(16, 128))

    place_in = lax.broadcasted_iota(jnp.int32, (1024, 1), 0)
    i, e, f = place_in // 128, (place_in // 16) % 8, place_in % 16
    perm = (e * 128 + i * 16 + f == lax.broadcasted_iota(jnp.int32, (1, 1024), 1)).astype(BF)
    slices = pl.pallas_call(
        slice_kernel,
        out_shape=[jax.ShapeDtypeStruct((2, U, 1024), BF)] * Z,
        in_specs=[SMEM] + [VMEM] * 4,
        out_specs=[VMEM] * Z,
        scratch_shapes=[pltpu.VMEM((512, 1024), BF), pltpu.VMEM((Z, 2, U, 1024), BF)],
        compiler_params=PARAMS,
        cost_estimate=pl.CostEstimate(flops=2**30, bytes_accessed=2**22, transcendentals=0),
        name="slices",
    )(place, x, comp_a, comp_b, perm)
    came = [slices[0]] + [None] * 7

    def exchange(event, distances):
        held, event = after([slices[k] for k in distances], event)
        for k, v in zip(distances, held):
            came[k] = lax.ppermute(v, "emb", [(i, (i + k) % Z) for i in range(Z)])
        return event

    def arrived(event, distances):
        held, event = after([came[k] for k in distances], event)
        for k, v in zip(distances, held):
            came[k] = v
        return event

    up1, down1 = step(normed, normed)
    up1, down1 = exchange((up1, down1), (1, 7))
    up2, down2 = step(up1, down1)
    up2, down2 = exchange((up2, down2), (2, 6))
    up3, down3 = step(up2, down2)
    up3, down3 = arrived((up3, down3), (1, 7))
    up3, down3 = exchange((up3, down3), (3, 5))
    low, high = step(up3[: U // 2], down3[U // 2 :])
    low, high = arrived((low, high), (2, 6))
    hidden = pl.pallas_call(
        hidden_kernel,
        out_shape=jax.ShapeDtypeStruct((Z * U, 512), BF),
        in_specs=[SMEM] + [VMEM] * 11,
        out_specs=VMEM,
        scratch_shapes=[pltpu.VMEM((Z * U, N * K), BF)],
        compiler_params=PARAMS,
        name="hidden",
    )(place, normed, up1, up2, up3, down1, down2, down3, low, high, w_hidden, w_hidden_other)

    users = Z * U
    weights = w_own, w_other
    up1, down1 = step(hidden, hidden)
    sums = part(place, [(0, hidden)], weights, [])
    (up1, down1), sums = after((up1, down1), sums)
    up1, down1 = arrived((up1, down1), (3, 5))
    up1, down1 = exchange((up1, down1), (4,))
    up2, down2 = step(up1, down1)
    sums = part(place, [(7, up1), (1, down1)], weights, sums)
    (up2, down2), sums = after((up2, down2), sums)
    up3, down3 = step(up2, down2)
    sums = part(place, [(6, up2), (2, down2)], weights, sums)
    (up3, down3), sums = after((up3, down3), sums)
    up3, down3 = arrived((up3, down3), (4,))
    low, high = step(up3[: users // 2], down3[users // 2 :])
    sums = part(place, [(5, up3), (3, down3)], weights, sums)
    slices = came

    def all_of(*shape):
        return pl.BlockSpec(shape, lambda i, at: (0,) * len(shape))

    column = pl.BlockSpec((512, 512), lambda i, at: (0, lax.rem(at[0] + 4, Z)))
    s_own, s_other, totals = pl.pallas_call(
        out_kernel,
        grid_spec=pltpu.PrefetchScalarGridSpec(
            num_scalar_prefetch=1,
            grid=(1,),
            in_specs=[all_of(users // 2, 512)] * 2
            + [column] * 2
            + [all_of(users, 512)] * 2
            + [all_of(2, U, 1024)] * Z,
            out_specs=[all_of(users, 512)] * 2 + [all_of(64, users)],
        ),
        out_shape=[jax.ShapeDtypeStruct((users, 512), F32)] * 2
        + [jax.ShapeDtypeStruct((64, users), F32)],
        compiler_params=PARAMS,
        name="fm_out",
    )(place, low, high, *weights, *sums, *slices)

    for bit in (1, 2, 4):
        theirs = lax.ppermute(totals.astype(BF), "emb", [(i, i ^ bit) for i in range(Z)])
        totals = totals + theirs.astype(F32)

    o_own, o_other = pl.pallas_call(
        scale_kernel,
        out_shape=[jax.ShapeDtypeStruct((users, 1024), BF)] * 2,
        in_specs=[SMEM] + [VMEM] * (3 + Z),
        out_specs=[VMEM] * 2,
        compiler_params=PARAMS,
        name="scale",
    )(place, s_own, s_other, totals, *slices)
    came = lax.ppermute(o_other, "section", SWAP)
    o_own, came = o_own.reshape(Z, 1, U, 1024), came.reshape(Z, 1, U, 1024)
    send = jnp.where(
        c == 0, jnp.concatenate([o_own, came], axis=1), jnp.concatenate([came, o_own], axis=1)
    )
    out = lax.all_to_all(send.reshape(16, U, 1024), "dp", 0, 0, tiled=True)
    gain = jnp.tile(out_gain, 64).reshape(1024, 1)
    out = pl.pallas_call(
        finish_kernel,
        out_shape=jax.ShapeDtypeStruct((1024, 512), BF),
        in_specs=[VMEM] * 2,
        out_specs=VMEM,
        compiler_params=PARAMS,
        name="finish",
    )(out.reshape(512, 1024), gain)
    return jnp.transpose(out.reshape(64, 16, 512), (2, 0, 1))


def solution(mesh):
    in_specs = (
        P(("emb", "section"), "dp", None, None),
        P(("emb", "section"), "dp"),
        P(("emb", "section"), "dp"),
        P(),
        P(),
        P(),
        P(None, ("emb", "section")),
        P(None, None, ("emb", "section")),
        P(),
        P(("emb", "section")),
    )
    out_specs = P("dp", None, ("emb", "section"))
    return jax.shard_map(shards, mesh=mesh, in_specs=in_specs, out_specs=out_specs, check_vma=False)
```

```python
import functools

import jax
import jax.numpy as jnp
from jax import lax
from jax.experimental import pallas as pl
from jax.experimental.pallas import tpu as pltpu
from jax.sharding import PartitionSpec as P

D = 256
N = 64
K = 32
U = 32
Z = 8
F32 = jnp.float32
BF = jnp.bfloat16
VMEM = pl.BlockSpec(memory_space=pltpu.VMEM)
SMEM = pl.BlockSpec(memory_space=pltpu.SMEM)
PARAMS = pltpu.CompilerParams(vmem_limit_bytes=24 * 1024 * 1024)
UP = [(i, (i + 1) % Z) for i in range(Z)]
DOWN = [(i, (i - 1) % Z) for i in range(Z)]
SWAP = [(0, 1), (1, 0)]
LANES = ((1,), (1,)), ((), ())


def dot_t(a, b):
    return lax.dot_general(a, b, LANES, preferred_element_type=F32)


def fm_kernel(x_ref, proj_ref, gain_ref, normed_ref, xa, xb, ts):
    xa[...] = x_ref[:, :128].astype(F32)
    xb[...] = x_ref[:, 128:].astype(F32)
    for u in range(U):
        sides = [
            jnp.concatenate(
                [xs[pl.ds(first * U + u, 16, stride=4 * U), :] for first in range(4)], axis=0
            )
            for xs in (xa, xb)
        ]
        xu = jnp.concatenate(sides, axis=1).astype(BF)
        reduced = jnp.dot(proj_ref[...], xu, preferred_element_type=F32).astype(BF)
        fm = dot_t(xu, reduced)
        ts[pl.ds(u, 16, stride=U), :] = jnp.concatenate(
            [fm[16 * i : 16 * i + 16] for i in range(4)], axis=1
        )
    t = ts[...].reshape(16, U, 128)
    m = jnp.sum(jnp.sum(t, axis=0), axis=-1, keepdims=True) / (N * K)
    q = jnp.sum(jnp.sum(t * t, axis=0), axis=-1, keepdims=True) / (N * K)
    scale = lax.rsqrt(q - m * m + 1e-05)
    for g in range(16):
        normed_ref[:, g * 128 : g * 128 + 128] = (
            (t[g] - m) * scale * gain_ref[g : g + 1, :]
        ).astype(BF)


def cut_kernel(at_ref, s_ref, perm_ref, own_ref, other_ref, cut, made):
    z, c = at_ref[0], at_ref[1]
    for t in range(2):
        for s in range(4):
            cut[t * 512 : t * 512 + 512, s * 128 : s * 128 + 128] = s_ref[
                s, :, t * 128 : t * 128 + 128
            ]
    made[...] = jnp.dot(cut[...], perm_ref[...], preferred_element_type=F32).astype(BF)
    for t in range(2):
        for side, ref in ((c, own_ref), (1 - c, other_ref)):
            rows = pl.ds(pl.multiple_of(t * 512 + side * 256, 256), 256)
            for q in range(4):
                ref[lax.rem(t * 4 + q + Z - z, Z)] = made[rows, q * 128 : q * 128 + 128]


def pair_kernel(own_ref, other_ref, *refs):
    for k, ref in enumerate(refs):
        ref[0] = own_ref[k]
        ref[1] = other_ref[k]


def pack_kernel(at_ref, *refs):
    came, out_ref = refs[:Z], refs[Z]
    z, c = at_ref[0], at_ref[1]
    for k, ref in enumerate(came):
        source = lax.rem(z + Z - k, Z)
        out_ref[2 * source + c] = ref[0]
        out_ref[2 * source + 1 - c] = ref[1]


def spread_kernel(lcb_ref, out_ref):
    rows = lax.broadcasted_iota(jnp.int32, (1024, 64), 0) // 16
    wide = (rows == lax.broadcasted_iota(jnp.int32, (1024, 64), 1)).astype(BF)
    cols = lax.broadcasted_iota(jnp.int32, (32, 512), 1) // 16
    long = (cols == lax.broadcasted_iota(jnp.int32, (32, 512), 0)).astype(BF)
    v = dot_t(wide, lcb_ref[...]).astype(BF)
    v = jnp.dot(v, long, preferred_element_type=F32)
    same = (
        lax.broadcasted_iota(jnp.int32, (1024, 512), 0) % 16
        == lax.broadcasted_iota(jnp.int32, (1024, 512), 1) % 16
    )
    out_ref[...] = jnp.where(same, v, 0.0).astype(BF)


def sums_of(x, y):
    mask = (
        lax.broadcasted_iota(jnp.int32, (32, 512), 1) // 16
        == lax.broadcasted_iota(jnp.int32, (32, 512), 0)
    ).astype(BF)
    parts = []
    for v in (x + y, x * x + y * y):
        upper = v.astype(BF)
        rest = (v - upper.astype(F32)).astype(BF)
        parts.append(dot_t(mask, upper) + dot_t(mask, rest))
    return jnp.concatenate(parts, axis=0)


def base_kernel(at_ref, s_ref, perm_ref, lcb_ref, f_own, f_other, c_own, c_other, tot_ref, made):
    c = at_ref[1]
    for p in range(8):
        pair = jnp.concatenate([s_ref[2 * p], s_ref[2 * p + 1]], axis=1)
        v = jnp.dot(pair, perm_ref[...], preferred_element_type=F32).astype(BF)
        made[0, :, p * 128 : p * 128 + 128] = v[:, :128]
        made[1, :, p * 128 : p * 128 + 128] = v[:, 128:]
    for side, f, o in ((c, f_own, c_own), (1 - c, f_other, c_other)):
        v = made[side]
        f[...] = v[:, :512]
        o[...] = v[:, 512:].astype(F32) + jnp.dot(v, lcb_ref[...], preferred_element_type=F32)
    tot_ref[...] = sums_of(c_own[...], c_other[...])


def hidden_kernel(at_ref, *refs):
    chunks, (own, other, out_ref, held) = refs[:9], refs[9:]
    z, c = at_ref[0], at_ref[1]
    for k, ref in zip((0, 7, 6, 5, 1, 2, 3), chunks[:7]):
        held[pl.ds(pl.multiple_of(lax.rem(z + k, Z) * U, U), U), :] = ref[...]
    half = pl.multiple_of(lax.rem(z + 4, Z) * U, U)
    held[pl.ds(half, U // 2), :] = chunks[7][...]
    held[pl.ds(half + U // 2, U // 2), :] = chunks[8][...]
    for where, w in ((c, own), (1 - c, other)):
        h = jnp.dot(held[...], w[...], preferred_element_type=F32)
        out_ref[:, pl.ds(pl.multiple_of(where * 256, 256), 256)] = jnp.maximum(h, 0.0).astype(BF)


def part_kernel(n, at_ref, *refs):
    chunks, weights = refs[:n], refs[n : 3 * n]
    sums, outs = refs[3 * n : -2], refs[-2:]
    for side, out in enumerate(outs):
        acc = sum(dot_t(chunks[i][...], weights[2 * i + side][...]) for i in range(n))
        out[...] = acc + sums[side][...] if sums else acc


def part(place, blocks, weights, sums):
    n = len(blocks)

    def columns(k):
        return pl.BlockSpec((512, 512), lambda i, at: (0, lax.rem(at[0] + k, Z)))

    whole = pl.BlockSpec((Z * U, 512), lambda i, at: (0, 0))
    return pl.pallas_call(
        functools.partial(part_kernel, n),
        grid_spec=pltpu.PrefetchScalarGridSpec(
            num_scalar_prefetch=1,
            grid=(1,),
            in_specs=[whole] * n
            + [columns(k) for k, _ in blocks for _ in range(2)]
            + [whole] * len(sums),
            out_specs=[whole] * 2,
        ),
        out_shape=[jax.ShapeDtypeStruct((Z * U, 512), F32)] * 2,
        compiler_params=PARAMS,
        cost_estimate=pl.CostEstimate(
            flops=n * 2 * 2 * 256 * 512 * 512, bytes_accessed=n * 2**20, transcendentals=0
        ),
        name="fm_out_part",
    )(place, *[v for _, v in blocks], *[w for _ in blocks for w in weights], *sums)


def out_kernel(
    at_ref, low, high, w_own, w_other, a_own, a_other, s_own, s_other, tc_ref, o_own, o_other, tot_ref
):
    half = low.shape[0]
    for w, a, s, o in ((w_own, a_own, s_own, o_own), (w_other, a_other, s_other, o_other)):
        o[:half] = a[:half] + s[:half].astype(F32) + dot_t(low[...], w[...])
        o[half:] = a[half:] + s[half:].astype(F32) + dot_t(high[...], w[...])
    tot_ref[:64] = sums_of(o_own[...], o_other[...])
    tot_ref[64:] = tc_ref[...]


def scale_kernel(f_own, f_other, c_own, c_other, tot_ref, o_own, o_other):
    spread = (
        lax.broadcasted_iota(jnp.int32, (32, 512), 1) // 16
        == lax.broadcasted_iota(jnp.int32, (32, 512), 0)
    ).astype(BF)

    def widen(v):
        high = v.astype(BF)
        low = (v - high.astype(F32)).astype(BF)
        dims = ((0,), (0,)), ((), ())
        return lax.dot_general(high, spread, dims, preferred_element_type=F32) + lax.dot_general(
            low, spread, dims, preferred_element_type=F32
        )

    for at, own, other in ((0, f_own, f_other), (64, c_own, c_other)):
        m = tot_ref[at : at + 32, :] / D
        q = tot_ref[at + 32 : at + 64, :] / D
        r = widen(lax.rsqrt(q - m * m + 1e-05))
        m = widen(m)
        for s, o in ((own, o_own), (other, o_other)):
            o[:, at * 8 : at * 8 + 512] = ((s[...] - m) * r).astype(BF)


def finish_kernel(at_ref, own_ref, came_ref, gain_ref, o_ref):
    c = at_ref[1]
    for side, ref in ((c, own_ref), (1 - c, came_ref)):
        v = ref[...].astype(F32).T * gain_ref[...]
        o_ref[:, pl.ds(pl.multiple_of(side * 256, 256), 256)] = v.astype(BF)


def step(up, down):
    return lax.ppermute(up, "emb", UP), lax.ppermute(down, "emb", DOWN)


def after(value, event):
    return lax.optimization_barrier((value, event))


def shards(
    events, counts, live, enc_weight, fm_proj, ln_gain, w_hidden, w_out, lcb_weight, out_gain
):
    users_enc, sess_dev, slot_count, full_width = events.shape
    z, c = lax.axis_index("emb"), lax.axis_index("section")
    place = jnp.stack([z, c]).astype(jnp.int32)
    w_hidden_other = lax.ppermute(w_hidden, "section", SWAP)
    w_own = jnp.transpose(w_out, (1, 2, 0)).reshape(512, -1)
    w_other = lax.ppermute(w_own, "section", SWAP)

    inside = (lax.broadcasted_iota(jnp.int32, (1, 1, slot_count), 2) < counts[:, :, None]).astype(BF)
    session_sums = jnp.einsum("usj,usjd->usd", inside, events, preferred_element_type=F32)
    share_of = live.astype(F32) / counts.astype(F32)
    pooled = (session_sums * share_of[:, :, None]).astype(BF)
    encoded = jnp.dot(pooled.reshape(-1, full_width), enc_weight, preferred_element_type=F32)
    session = encoded.reshape(users_enc, sess_dev, full_width).astype(BF)
    chunks = jnp.transpose(session.reshape(2, Z, U, sess_dev, D), (1, 0, 3, 2, 4))
    x = lax.all_to_all(chunks.reshape(16, sess_dev, U, D), "dp", 0, 0, tiled=True)
    x = x.reshape(N * U, D)

    def call(kernel, name, shapes, args, scratch=(), scalars=(place,), flops=2**28):
        return pl.pallas_call(
            kernel,
            out_shape=[jax.ShapeDtypeStruct(*v) for v in shapes],
            in_specs=[SMEM] * len(scalars) + [VMEM] * len(args),
            out_specs=[VMEM] * len(shapes),
            scratch_shapes=scratch,
            compiler_params=PARAMS,
            cost_estimate=pl.CostEstimate(flops=flops, bytes_accessed=2**22, transcendentals=0),
            name=name,
        )(*scalars, *args)

    row = lax.broadcasted_iota(jnp.int32, (512, 1), 0)
    goal = (row // 32) % 4 * 128 + (row // 16) % 2 * 64 + row // 128 * 16 + row % 16
    perm = (goal == lax.broadcasted_iota(jnp.int32, (1, 512), 1)).astype(BF)
    own, other = call(
        cut_kernel,
        "cut",
        [((Z, 256, 128), BF)] * 2,
        (jnp.transpose(session, (1, 0, 2)), perm),
        [pltpu.VMEM((1024, 512), BF)] * 2,
    )
    other = lax.ppermute(other, "section", SWAP)
    slices = call(pair_kernel, "pair", [((2, 256, 128), BF)] * Z, (own, other), scalars=())
    came = [slices[0]] + [None] * 7
    for k in (1, 7, 2, 6, 3, 5, 4):
        came[k] = lax.ppermute(slices[k], "emb", [(i, (i + k) % Z) for i in range(Z)])

    def arrived(event, distances):
        held, event = after([came[k] for k in distances], event)
        for k, v in zip(distances, held):
            came[k] = v
        return event

    x = arrived(x, (1, 7))
    row = lax.broadcasted_iota(jnp.int32, (256, 1), 0)
    goal = (row // 64) % 2 * 128 + row // 128 * 64 + row % 64
    perm = (goal == lax.broadcasted_iota(jnp.int32, (1, 256), 1)).astype(BF)
    (spread,) = call(spread_kernel, "spread", [((1024, 512), BF)], (lcb_weight,), scalars=())

    proj = jnp.transpose(fm_proj.T.reshape(K, 16, 4), (0, 2, 1)).reshape(K, N)
    (normed,) = call(
        fm_kernel,
        "fm_rows",
        [((U, N * K), BF)],
        (x, proj, ln_gain.reshape(16, 128)),
        [pltpu.VMEM((N * U, 128), F32)] * 2 + [pltpu.VMEM((16 * U, 128), F32)],
        scalars=(),
    )
    normed = arrived(normed, (2, 6, 3, 5))
    normed = lax.ppermute(
        normed,
        ("dp", "emb", "section"),
        [(a * 16 + b, b * 16 + a) for a in range(16) for b in range(16)],
    )
    normed = arrived(normed, (4,))
    up1, down1 = step(normed, normed)
    came[0], _ = after(came[0], (up1, down1))
    (packed,) = call(pack_kernel, "pack", [((16, 256, 128), BF)], tuple(came))
    slices = lax.all_to_all(packed, "dp", 0, 0, tiled=True)
    up2, down2 = step(up1, down1)
    up3, down3 = step(up2, down2)
    low, high = step(up3[: U // 2], down3[U // 2 :])
    hidden = pl.pallas_call(
        hidden_kernel,
        out_shape=jax.ShapeDtypeStruct((Z * U, 512), BF),
        in_specs=[SMEM] + [VMEM] * 11,
        out_specs=VMEM,
        scratch_shapes=[pltpu.VMEM((Z * U, N * K), BF)],
        compiler_params=PARAMS,
        name="hidden",
    )(place, normed, up1, up2, up3, down1, down2, down3, low, high, w_hidden, w_hidden_other)

    users = Z * U
    weights = w_own, w_other
    up1, down1 = step(hidden, hidden)
    sums = part(place, [(0, hidden)], weights, [])
    f_own, f_other, c_own, c_other, c_sums = call(
        base_kernel,
        "base",
        [((users, 512), BF)] * 2 + [((users, 512), F32)] * 2 + [((64, users), F32)],
        (slices, perm, spread),
        [pltpu.VMEM((2, users, 1024), BF)],
    )
    (up1, down1), sums = after((up1, down1), sums)
    (up1, down1), (f_own, f_other) = after((up1, down1), (f_own, f_other))
    up2, down2 = step(up1, down1)
    sums = part(place, [(7, up1), (1, down1)], weights, sums)
    (up2, down2), sums = after((up2, down2), sums)
    up3, down3 = step(up2, down2)
    sums = part(place, [(6, up2), (2, down2)], weights, sums)
    (up3, down3), sums = after((up3, down3), sums)
    low, high = step(up3[: users // 2], down3[users // 2 :])
    sums = part(place, [(5, up3), (3, down3)], weights, sums)

    def all_of(*shape):
        return pl.BlockSpec(shape, lambda i, at: (0,) * len(shape))

    column = pl.BlockSpec((512, 512), lambda i, at: (0, lax.rem(at[0] + 4, Z)))
    f_own, f_other, totals = pl.pallas_call(
        out_kernel,
        grid_spec=pltpu.PrefetchScalarGridSpec(
            num_scalar_prefetch=1,
            grid=(1,),
            in_specs=[all_of(users // 2, 512)] * 2
            + [column] * 2
            + [all_of(users, 512)] * 4
            + [all_of(64, users)],
            out_specs=[all_of(users, 512)] * 2 + [all_of(128, users)],
        ),
        out_shape=[jax.ShapeDtypeStruct((users, 512), F32)] * 2
        + [jax.ShapeDtypeStruct((128, users), F32)],
        compiler_params=PARAMS,
        name="fm_out",
    )(place, low, high, *weights, *sums, f_own, f_other, c_sums)

    for bit in (1, 2, 4):
        theirs = lax.ppermute(totals.astype(BF), "emb", [(i, i ^ bit) for i in range(Z)])
        totals = totals + theirs.astype(F32)

    own, other = call(
        scale_kernel,
        "scale",
        [((users, 1024), BF)] * 2,
        (f_own, f_other, c_own, c_other, totals),
        scalars=(),
    )
    other = lax.ppermute(other, "section", SWAP)
    gain = jnp.tile(out_gain, 64).reshape(1024, 1)
    (out,) = call(finish_kernel, "finish", [((1024, 512), BF)], (own, other, gain))
    return jnp.transpose(out.reshape(64, 16, 512), (2, 0, 1))


def solution(mesh):
    in_specs = (
        P(("emb", "section"), "dp", None, None),
        P(("emb", "section"), "dp"),
        P(("emb", "section"), "dp"),
        P(),
        P(),
        P(),
        P(None, ("emb", "section")),
        P(None, None, ("emb", "section")),
        P(),
        P(("emb", "section")),
    )
    out_specs = P("dp", None, ("emb", "section"))
    return jax.shard_map(shards, mesh=mesh, in_specs=in_specs, out_specs=out_specs, check_vma=False)
```

```python
import functools

import jax
import jax.numpy as jnp
from jax import lax
from jax.experimental import pallas as pl
from jax.experimental.pallas import tpu as pltpu
from jax.sharding import PartitionSpec as P

D = 256
N = 64
K = 32
U = 32
Z = 8
F32 = jnp.float32
BF = jnp.bfloat16
VMEM = pl.BlockSpec(memory_space=pltpu.VMEM)
SMEM = pl.BlockSpec(memory_space=pltpu.SMEM)
PARAMS = pltpu.CompilerParams(vmem_limit_bytes=24 * 1024 * 1024)
UP = [(i, (i + 1) % Z) for i in range(Z)]
DOWN = [(i, (i - 1) % Z) for i in range(Z)]
SWAP = [(0, 1), (1, 0)]
LANES = ((1,), (1,)), ((), ())


def dot_t(a, b):
    return lax.dot_general(a, b, LANES, preferred_element_type=F32)


def fm_kernel(x_ref, proj_ref, gain_ref, normed_ref, xa, xb, ts):
    xa[...] = x_ref[:, :128].astype(F32)
    xb[...] = x_ref[:, 128:].astype(F32)
    for u in range(U):
        sides = [
            jnp.concatenate(
                [xs[pl.ds(first * U + u, 16, stride=4 * U), :] for first in range(4)], axis=0
            )
            for xs in (xa, xb)
        ]
        xu = jnp.concatenate(sides, axis=1).astype(BF)
        reduced = jnp.dot(proj_ref[...], xu, preferred_element_type=F32).astype(BF)
        fm = dot_t(xu, reduced)
        ts[pl.ds(u, 16, stride=U), :] = jnp.concatenate(
            [fm[16 * i : 16 * i + 16] for i in range(4)], axis=1
        )
    t = ts[...].reshape(16, U, 128)
    m = jnp.sum(jnp.sum(t, axis=0), axis=-1, keepdims=True) / (N * K)
    q = jnp.sum(jnp.sum(t * t, axis=0), axis=-1, keepdims=True) / (N * K)
    scale = lax.rsqrt(q - m * m + 1e-05)
    for g in range(16):
        normed_ref[:, g * 128 : g * 128 + 128] = (
            (t[g] - m) * scale * gain_ref[g : g + 1, :]
        ).astype(BF)


def cut_kernel(at_ref, s_ref, perm_ref, own_ref, other_ref, cut, made):
    z, c = at_ref[0], at_ref[1]
    for t in range(2):
        for s in range(4):
            cut[t * 512 : t * 512 + 512, s * 128 : s * 128 + 128] = s_ref[
                s, :, t * 128 : t * 128 + 128
            ]
    made[...] = jnp.dot(cut[...], perm_ref[...], preferred_element_type=F32).astype(BF)
    for t in range(2):
        for side, ref in ((c, own_ref), (1 - c, other_ref)):
            rows = pl.ds(pl.multiple_of(t * 512 + side * 256, 256), 256)
            for q in range(4):
                ref[lax.rem(t * 4 + q + Z - z, Z)] = made[rows, q * 128 : q * 128 + 128]


def pair_kernel(own_ref, other_ref, *refs):
    for k, ref in enumerate(refs):
        ref[0] = own_ref[k]
        ref[1] = other_ref[k]


def pack_kernel(at_ref, *refs):
    came, out_ref = refs[:Z], refs[Z]
    z, c = at_ref[0], at_ref[1]
    for k, ref in enumerate(came):
        source = lax.rem(z + Z - k, Z)
        out_ref[2 * source + c] = ref[0]
        out_ref[2 * source + 1 - c] = ref[1]


def spread_kernel(lcb_ref, out_ref):
    rows = lax.broadcasted_iota(jnp.int32, (1024, 64), 0) // 16
    wide = (rows == lax.broadcasted_iota(jnp.int32, (1024, 64), 1)).astype(BF)
    cols = lax.broadcasted_iota(jnp.int32, (32, 512), 1) // 16
    long = (cols == lax.broadcasted_iota(jnp.int32, (32, 512), 0)).astype(BF)
    v = dot_t(wide, lcb_ref[...]).astype(BF)
    v = jnp.dot(v, long, preferred_element_type=F32)
    same = (
        lax.broadcasted_iota(jnp.int32, (1024, 512), 0) % 16
        == lax.broadcasted_iota(jnp.int32, (1024, 512), 1) % 16
    )
    out_ref[...] = jnp.where(same, v, 0.0).astype(BF)


def sums_of(x, y):
    mask = (
        lax.broadcasted_iota(jnp.int32, (32, 512), 1) // 16
        == lax.broadcasted_iota(jnp.int32, (32, 512), 0)
    ).astype(BF)
    parts = []
    for v in (x + y, x * x + y * y):
        upper = v.astype(BF)
        rest = (v - upper.astype(F32)).astype(BF)
        parts.append(dot_t(mask, upper) + dot_t(mask, rest))
    return jnp.concatenate(parts, axis=0)


def base_kernel(at_ref, s_ref, perm_ref, lcb_ref, f_own, f_other, c_own, c_other, tot_ref, made):
    c = at_ref[1]
    for p in range(8):
        pair = jnp.concatenate([s_ref[2 * p], s_ref[2 * p + 1]], axis=1)
        v = jnp.dot(pair, perm_ref[...], preferred_element_type=F32).astype(BF)
        made[0, :, p * 128 : p * 128 + 128] = v[:, :128]
        made[1, :, p * 128 : p * 128 + 128] = v[:, 128:]
    for side, f, o in ((c, f_own, c_own), (1 - c, f_other, c_other)):
        v = made[side]
        f[...] = v[:, :512]
        o[...] = v[:, 512:].astype(F32) + jnp.dot(v, lcb_ref[...], preferred_element_type=F32)
    tot_ref[...] = sums_of(c_own[...], c_other[...])


def hidden_kernel(at_ref, *refs):
    chunks, (own, other, out_ref, held) = refs[:9], refs[9:]
    z, c = at_ref[0], at_ref[1]
    for k, ref in zip((0, 7, 6, 5, 1, 2, 3), chunks[:7]):
        held[pl.ds(pl.multiple_of(lax.rem(z + k, Z) * U, U), U), :] = ref[...]
    half = pl.multiple_of(lax.rem(z + 4, Z) * U, U)
    held[pl.ds(half, U // 2), :] = chunks[7][...]
    held[pl.ds(half + U // 2, U // 2), :] = chunks[8][...]
    for where, w in ((c, own), (1 - c, other)):
        h = jnp.dot(held[...], w[...], preferred_element_type=F32)
        out_ref[:, pl.ds(pl.multiple_of(where * 256, 256), 256)] = jnp.maximum(h, 0.0).astype(BF)


def part_kernel(n, at_ref, *refs):
    chunks, weights = refs[:n], refs[n : 3 * n]
    sums, outs = refs[3 * n : -2], refs[-2:]
    for side, out in enumerate(outs):
        acc = sum(dot_t(chunks[i][...], weights[2 * i + side][...]) for i in range(n))
        out[...] = acc + sums[side][...] if sums else acc


def part(place, blocks, weights, sums):
    n = len(blocks)

    def columns(k):
        return pl.BlockSpec((512, 512), lambda i, at: (0, lax.rem(at[0] + k, Z)))

    whole = pl.BlockSpec((Z * U, 512), lambda i, at: (0, 0))
    return pl.pallas_call(
        functools.partial(part_kernel, n),
        grid_spec=pltpu.PrefetchScalarGridSpec(
            num_scalar_prefetch=1,
            grid=(1,),
            in_specs=[whole] * n
            + [columns(k) for k, _ in blocks for _ in range(2)]
            + [whole] * len(sums),
            out_specs=[whole] * 2,
        ),
        out_shape=[jax.ShapeDtypeStruct((Z * U, 512), F32)] * 2,
        compiler_params=PARAMS,
        cost_estimate=pl.CostEstimate(
            flops=n * 2 * 2 * 256 * 512 * 512, bytes_accessed=n * 2**20, transcendentals=0
        ),
        name="fm_out_part",
    )(place, *[v for _, v in blocks], *[w for _ in blocks for w in weights], *sums)


def out_kernel(
    at_ref, low, high, w_own, w_other, a_own, a_other, s_own, s_other, tc_ref, o_own, o_other, tot_ref
):
    half = low.shape[0]
    for w, a, s, o in ((w_own, a_own, s_own, o_own), (w_other, a_other, s_other, o_other)):
        o[:half] = a[:half] + s[:half].astype(F32) + dot_t(low[...], w[...])
        o[half:] = a[half:] + s[half:].astype(F32) + dot_t(high[...], w[...])
    tot_ref[:64] = sums_of(o_own[...], o_other[...])
    tot_ref[64:] = tc_ref[...]


def scale_kernel(f_own, f_other, c_own, c_other, tot_ref, o_own, o_other):
    spread = (
        lax.broadcasted_iota(jnp.int32, (32, 512), 1) // 16
        == lax.broadcasted_iota(jnp.int32, (32, 512), 0)
    ).astype(BF)

    def widen(v):
        high = v.astype(BF)
        low = (v - high.astype(F32)).astype(BF)
        dims = ((0,), (0,)), ((), ())
        return lax.dot_general(high, spread, dims, preferred_element_type=F32) + lax.dot_general(
            low, spread, dims, preferred_element_type=F32
        )

    for at, own, other in ((0, f_own, f_other), (64, c_own, c_other)):
        m = tot_ref[at : at + 32, :] / D
        q = tot_ref[at + 32 : at + 64, :] / D
        r = widen(lax.rsqrt(q - m * m + 1e-05))
        m = widen(m)
        for s, o in ((own, o_own), (other, o_other)):
            o[:, at * 8 : at * 8 + 512] = ((s[...] - m) * r).astype(BF)


def finish_kernel(at_ref, own_ref, came_ref, gain_ref, o_ref):
    c = at_ref[1]
    for side, ref in ((c, own_ref), (1 - c, came_ref)):
        v = ref[...].astype(F32).T * gain_ref[...]
        o_ref[:, pl.ds(pl.multiple_of(side * 256, 256), 256)] = v.astype(BF)


def step(up, down):
    return lax.ppermute(up, "emb", UP), lax.ppermute(down, "emb", DOWN)


def after(value, event):
    return lax.optimization_barrier((value, event))


def shards(
    events, counts, live, enc_weight, fm_proj, ln_gain, w_hidden, w_out, lcb_weight, out_gain
):
    users_enc, sess_dev, slot_count, full_width = events.shape
    z, c = lax.axis_index("emb"), lax.axis_index("section")
    place = jnp.stack([z, c]).astype(jnp.int32)
    w_hidden_other = lax.ppermute(w_hidden, "section", SWAP)
    w_own = jnp.transpose(w_out, (1, 2, 0)).reshape(512, -1)
    w_other = lax.ppermute(w_own, "section", SWAP)

    inside = (lax.broadcasted_iota(jnp.int32, (1, 1, slot_count), 2) < counts[:, :, None]).astype(BF)
    session_sums = jnp.einsum("usj,usjd->usd", inside, events, preferred_element_type=F32)
    share_of = live.astype(F32) / counts.astype(F32)
    pooled = (session_sums * share_of[:, :, None]).astype(BF)
    encoded = jnp.dot(pooled.reshape(-1, full_width), enc_weight, preferred_element_type=F32)
    session = encoded.reshape(users_enc, sess_dev, full_width).astype(BF)
    chunks = jnp.transpose(session.reshape(2, Z, U, sess_dev, D), (1, 0, 3, 2, 4))
    chunks = chunks.reshape(16, sess_dev, U, D)
    chunks = lax.dynamic_slice_in_dim(jnp.concatenate([chunks, chunks], axis=0), 2 * z + c, 16)
    x = lax.all_to_all(chunks, "dp", 0, 0, tiled=True)
    x = x.reshape(N * U, D)

    def call(kernel, name, shapes, args, scratch=(), scalars=(place,), flops=2**28):
        return pl.pallas_call(
            kernel,
            out_shape=[jax.ShapeDtypeStruct(*v) for v in shapes],
            in_specs=[SMEM] * len(scalars) + [VMEM] * len(args),
            out_specs=[VMEM] * len(shapes),
            scratch_shapes=scratch,
            compiler_params=PARAMS,
            cost_estimate=pl.CostEstimate(flops=flops, bytes_accessed=2**22, transcendentals=0),
            name=name,
        )(*scalars, *args)

    row = lax.broadcasted_iota(jnp.int32, (512, 1), 0)
    goal = (row // 32) % 4 * 128 + (row // 16) % 2 * 64 + row // 128 * 16 + row % 16
    perm = (goal == lax.broadcasted_iota(jnp.int32, (1, 512), 1)).astype(BF)
    own, other = call(
        cut_kernel,
        "cut",
        [((Z, 256, 128), BF)] * 2,
        (jnp.transpose(session, (1, 0, 2)), perm),
        [pltpu.VMEM((1024, 512), BF)] * 2,
    )
    other = lax.ppermute(other, "section", SWAP)
    slices = call(pair_kernel, "pair", [((2, 256, 128), BF)] * Z, (own, other), scalars=())
    came = [slices[0]] + [None] * 7
    for k in (1, 7, 2, 6, 3, 5, 4):
        came[k] = lax.ppermute(slices[k], "emb", [(i, (i + k) % Z) for i in range(Z)])

    def arrived(event, distances):
        held, event = after([came[k] for k in distances], event)
        for k, v in zip(distances, held):
            came[k] = v
        return event

    x = arrived(x, (1, 7))
    row = lax.broadcasted_iota(jnp.int32, (256, 1), 0)
    goal = (row // 64) % 2 * 128 + row // 128 * 64 + row % 64
    perm = (goal == lax.broadcasted_iota(jnp.int32, (1, 256), 1)).astype(BF)
    (spread,) = call(spread_kernel, "spread", [((1024, 512), BF)], (lcb_weight,), scalars=())

    proj = jnp.transpose(fm_proj.T.reshape(K, 16, 4), (0, 2, 1)).reshape(K, N)
    (normed,) = call(
        fm_kernel,
        "fm_rows",
        [((U, N * K), BF)],
        (x, proj, ln_gain.reshape(16, 128)),
        [pltpu.VMEM((N * U, 128), F32)] * 2 + [pltpu.VMEM((16 * U, 128), F32)],
        scalars=(),
    )
    normed = arrived(normed, (2, 6, 3, 5))
    normed = lax.ppermute(
        normed,
        ("dp", "emb", "section"),
        [(a * 16 + b, b * 16 + (a + b) % 16) for a in range(16) for b in range(16)],
    )
    normed = arrived(normed, (4,))
    up1, down1 = step(normed, normed)
    came[0], _ = after(came[0], (up1, down1))
    (packed,) = call(pack_kernel, "pack", [((16, 256, 128), BF)], tuple(came))
    slices = lax.all_to_all(packed, "dp", 0, 0, tiled=True)
    up2, down2 = step(up1, down1)
    up3, down3 = step(up2, down2)
    low, high = step(up3[: U // 2], down3[U // 2 :])
    hidden = pl.pallas_call(
        hidden_kernel,
        out_shape=jax.ShapeDtypeStruct((Z * U, 512), BF),
        in_specs=[SMEM] + [VMEM] * 11,
        out_specs=VMEM,
        scratch_shapes=[pltpu.VMEM((Z * U, N * K), BF)],
        compiler_params=PARAMS,
        name="hidden",
    )(place, normed, up1, up2, up3, down1, down2, down3, low, high, w_hidden, w_hidden_other)

    users = Z * U
    weights = w_own, w_other
    up1, down1 = step(hidden, hidden)
    sums = part(place, [(0, hidden)], weights, [])
    f_own, f_other, c_own, c_other, c_sums = call(
        base_kernel,
        "base",
        [((users, 512), BF)] * 2 + [((users, 512), F32)] * 2 + [((64, users), F32)],
        (slices, perm, spread),
        [pltpu.VMEM((2, users, 1024), BF)],
    )
    (up1, down1), sums = after((up1, down1), sums)
    (up1, down1), (f_own, f_other) = after((up1, down1), (f_own, f_other))
    up2, down2 = step(up1, down1)
    sums = part(place, [(7, up1), (1, down1)], weights, sums)
    (up2, down2), sums = after((up2, down2), sums)
    up3, down3 = step(up2, down2)
    sums = part(place, [(6, up2), (2, down2)], weights, sums)
    (up3, down3), sums = after((up3, down3), sums)
    low, high = step(up3[: users // 2], down3[users // 2 :])
    sums = part(place, [(5, up3), (3, down3)], weights, sums)

    def all_of(*shape):
        return pl.BlockSpec(shape, lambda i, at: (0,) * len(shape))

    column = pl.BlockSpec((512, 512), lambda i, at: (0, lax.rem(at[0] + 4, Z)))
    f_own, f_other, totals = pl.pallas_call(
        out_kernel,
        grid_spec=pltpu.PrefetchScalarGridSpec(
            num_scalar_prefetch=1,
            grid=(1,),
            in_specs=[all_of(users // 2, 512)] * 2
            + [column] * 2
            + [all_of(users, 512)] * 4
            + [all_of(64, users)],
            out_specs=[all_of(users, 512)] * 2 + [all_of(128, users)],
        ),
        out_shape=[jax.ShapeDtypeStruct((users, 512), F32)] * 2
        + [jax.ShapeDtypeStruct((128, users), F32)],
        compiler_params=PARAMS,
        name="fm_out",
    )(place, low, high, *weights, *sums, f_own, f_other, c_sums)

    for bit in (1, 2, 4):
        theirs = lax.ppermute(totals.astype(BF), "emb", [(i, i ^ bit) for i in range(Z)])
        totals = totals + theirs.astype(F32)

    own, other = call(
        scale_kernel,
        "scale",
        [((users, 1024), BF)] * 2,
        (f_own, f_other, c_own, c_other, totals),
        scalars=(),
    )
    other = lax.ppermute(other, "section", SWAP)
    gain = jnp.tile(out_gain, 64).reshape(1024, 1)
    (out,) = call(finish_kernel, "finish", [((1024, 512), BF)], (own, other, gain))
    return jnp.transpose(out.reshape(64, 16, 512), (2, 0, 1))


def solution(mesh):
    in_specs = (
        P(("emb", "section"), "dp", None, None),
        P(("emb", "section"), "dp"),
        P(("emb", "section"), "dp"),
        P(),
        P(),
        P(),
        P(None, ("emb", "section")),
        P(None, None, ("emb", "section")),
        P(),
        P(("emb", "section")),
    )
    out_specs = P("dp", None, ("emb", "section"))
    return jax.shard_map(shards, mesh=mesh, in_specs=in_specs, out_specs=out_specs, check_vma=False)
```
